512 devices in a mesh: seq: 128 (over z, x, core), head: 4 (over y).
Axes of the slice: x: 4, y: 4, z: 16, core: 2. Of those that a mesh axis runs over, the one named last changes fastest.
Arguments:
- queries: bfloat16 [16384, 2560], P('seq', 'head'), may hold values from -6 to 6
- keys: bfloat16 [16384, 2560], P('seq', 'head'), may hold values from -6 to 6
- values: bfloat16 [16384, 2560], P('seq', 'head'), may hold values from -6 to 6
- head_class: int32 [20], replicated, may hold values from 0 to 1, as said below
- window_lengths: int32 [128, 4], P('seq'), may hold values from 1 to 64, 128 in all within a row
- out_weight: bfloat16 [2560, 5120], P('seq', 'head'), may hold values from -0.125 to 0.125
Outputs:
- projected: bfloat16 [16384, 5120], P('seq', 'head')
The draws below stay inside these ranges and needn't reach their ends.
Inputs may be any that keep to these rules, and one draw needn't show every extreme that they name: `head_class`: each group of 5 consecutive heads holds 1 to 3 temporal heads, and some group holds exactly 3. `window_lengths`: the 4 lengths of each block sum to 128, and the longest is exactly 64.
All inputs are finite; a program needn't handle non-finite values.
Results may differ from the reference program's by a relative error of at most 0.0057.
Values may be sent and summed in bfloat16 or wider, within the bound.
No kernel may reach another device: no remote copies, remote signals or barrier semaphores. Data moves between devices by JAX's collectives and lax.ppermute only.
A program may use at most 64 MiB of HBM per device.

```python
import math
import jax
import jax.numpy as jnp
import numpy as np
from jax import lax

D = 5120
HEADS = 20
HD = 128
TMAX = 3
NWIN = 4
FRAMES = 8
TOK_DEV = 128
WIN = 64
TOKENS = 16384
SPATIAL = 2048
BLOCKS = 128
N_HEAD = 4


def alternate(even_rows, odd_rows):
    return jnp.stack((even_rows, odd_rows), axis=1).reshape(TOKENS, HEADS * HD)


def draw_queries(key, part):
    key = jax.random.fold_in(key, 101)
    shape = (TOKENS // 2, HEADS * HD)
    even_key, odd_key = jax.random.split(key)
    even_rows = jnp.clip(jax.random.normal(even_key, shape), -4.5, 4.5)
    odd_rows = jnp.clip(jax.random.normal(odd_key, shape), -4.5, 4.5)
    return alternate(even_rows, odd_rows).astype(jnp.bfloat16)


def draw_keys(key, part):
    key = jax.random.fold_in(key, 202)
    shape = (TOKENS // 2, HEADS * HD)
    even_key, odd_key = jax.random.split(key)
    even_rows = jnp.clip(jax.random.normal(even_key, shape), -4.5, 4.5)
    odd_rows = jnp.clip(jax.random.normal(odd_key, shape), -4.5, 4.5)
    return alternate(even_rows, odd_rows).astype(jnp.bfloat16)


def draw_head_class(key, part):
    key = jax.random.fold_in(key, 303)
    count_key, full_key, order_key = jax.random.split(key, 3)
    per_group = HEADS // N_HEAD
    counts = jax.random.randint(count_key, (N_HEAD,), 1, TMAX + 1)
    full_group = jax.random.randint(full_key, (), 0, N_HEAD)
    counts = jnp.where(jnp.arange(N_HEAD, dtype=jnp.int32) == full_group, TMAX, counts)
    group_keys = jax.random.split(order_key, N_HEAD)
    orders = jax.vmap(lambda group_key: jax.random.permutation(group_key, per_group))(group_keys)
    return (orders < counts[:, None]).astype(jnp.int32).reshape(HEADS)


def block_scale(own_key, extent, cuts, smallest, largest):
    gain = 1.0
    for dim, blocks in cuts:
        draws = jax.random.uniform(jax.random.fold_in(jax.random.fold_in(own_key, 6), dim), (blocks,), jnp.float32, smallest / len(cuts), largest / len(cuts))
        gain = gain * jnp.repeat(jnp.exp(draws), extent[dim] // blocks).reshape((-1,) + (1,) * (len(extent) - 1 - dim))
    return gain


def length_profile(amount, total, reach, skew):
    weights = [(1 << 20) // math.isqrt(grade ** skew) + 1 for grade in range(2, amount + 1)]
    surplus, given = total - reach - (amount - 1), [1] * (amount - 1)
    while surplus > 0:
        candidates = [i for i in range(amount - 1) if given[i] < reach]
        pool, budget = sum([weights[i] for i in candidates]), surplus
        for i in candidates:
            extra = min(reach - given[i], max(1, budget * weights[i] // pool), surplus)
            given[i] = given[i] + extra
            surplus = surplus - extra
    return np.array([reach] + given)


def uneven_parts(rng, count, total, most, lean):
    if count == 2:
        one = jax.random.randint(rng, (), max(1, total - most), min(most, total - 1) + 1)
        return jnp.stack([one, total - one])
    tallies = jnp.asarray(length_profile(count, total, most, lean), jnp.int32)
    couples = (count - 1) // 2
    donor, sink = tallies[1:1 + 2 * couples:2], tallies[2:2 + 2 * couples:2]
    margin = jnp.minimum(donor - 1, most - sink)
    passed = jax.random.randint(jax.random.fold_in(rng, 1), (couples,), 0, 1 << 20) % (margin + 1)
    tallies = tallies.at[1:1 + 2 * couples:2].set(donor - passed).at[2:2 + 2 * couples:2].set(sink + passed)
    return tallies[jax.random.permutation(jax.random.fold_in(rng, 2), count)]


def centred(key, dims, width, bound, cuts=(), held_as=jnp.bfloat16):
    level = block_scale(key, dims, cuts, -0.22, 0.18) if cuts else 1.0
    entries = jax.random.normal(key, dims, jnp.float32) * width * level
    return jnp.minimum(jnp.maximum(entries, -bound), bound).astype(held_as)


def setup_inputs(seed: int = 0) -> dict:
    arg_keys = jax.random.split(jax.random.key(seed), 7)
    return {
        "queries": draw_queries(jax.random.fold_in(arg_keys[6], 71), 0),
        "keys": draw_keys(jax.random.fold_in(arg_keys[6], 71), 0),
        "values": centred(arg_keys[2], (TOKENS, HEADS * HD), 1.0, 6.0, ((0, 128), (1, 4))),
        "head_class": draw_head_class(jax.random.fold_in(arg_keys[6], 71), 0),
        "window_lengths": jax.vmap(lambda own: uneven_parts(own, NWIN, TOK_DEV, WIN, 0))(jax.random.split(arg_keys[4], BLOCKS)).reshape((BLOCKS, NWIN)).astype(jnp.int32),
        "out_weight": centred(arg_keys[5], (HEADS * HD, D), (HEADS * HD) ** -0.5, 0.125, ((0, 128), (1, 4))),
    }


def softmax_rows(scores):
    highest = lax.optimization_barrier(jnp.max(scores, axis=-1, keepdims=True))
    weights = jnp.exp(scores - highest)
    return weights / lax.optimization_barrier(jnp.sum(weights, axis=-1, keepdims=True))

def spatial_block(inputs):
    query, key_rows, value_rows, lengths = inputs
    scaling = 1.0 / math.sqrt(HD)
    ends = jnp.cumsum(lengths)
    positions = jnp.arange(TOK_DEV, dtype=jnp.int32)
    window_ids = lax.optimization_barrier(jnp.sum((positions[:, None] >= ends[None, :]).astype(jnp.int32), axis=1))
    same_window = window_ids[:, None] == window_ids[None, :]
    query_wide = query.reshape(TOK_DEV, HEADS, HD).astype(jnp.float32)
    key_wide = key_rows.reshape(TOK_DEV, HEADS, HD).astype(jnp.float32)
    value_wide = value_rows.reshape(TOK_DEV, HEADS, HD).astype(jnp.float32)
    scores = jnp.einsum('shd,thd->hst', query_wide, key_wide) * scaling
    scores = jnp.where(same_window[None], scores, -1e+30)
    weights = softmax_rows(scores).astype(jnp.bfloat16)
    return jnp.einsum('hst,thd->shd', weights.astype(jnp.float32), value_wide).astype(jnp.bfloat16)

def reference(queries, keys, values, head_class, window_lengths, out_weight):
    scaling = 1.0 / math.sqrt(HD)
    blocks_total = TOKENS // TOK_DEV
    cols = HEADS * HD
    spatial_out = lax.map(spatial_block, (queries.reshape(blocks_total, TOK_DEV, cols), keys.reshape(blocks_total, TOK_DEV, cols), values.reshape(blocks_total, TOK_DEV, cols), window_lengths))
    spatial_out = spatial_out.reshape(FRAMES, SPATIAL, HEADS, HD)
    block_cols = 32
    framed_q = queries.reshape(FRAMES, SPATIAL, cols)
    framed_k = keys.reshape(FRAMES, SPATIAL, cols)
    framed_v = values.reshape(FRAMES, SPATIAL, cols)

    def temporal_block(first_col):

        def pick(source):
            taken = lax.dynamic_slice_in_dim(source, first_col, block_cols, 1)
            return taken.reshape(FRAMES, block_cols, HEADS, HD).astype(jnp.float32)
        query_wide = pick(framed_q)
        key_wide = pick(framed_k)
        value_wide = pick(framed_v)
        scores = jnp.einsum('fbhd,gbhd->bhfg', query_wide, key_wide) * scaling
        weights = softmax_rows(scores).astype(jnp.bfloat16)
        return jnp.einsum('bhfg,gbhd->fbhd', weights.astype(jnp.float32), value_wide).astype(jnp.bfloat16)
    starts = (jnp.arange(SPATIAL // block_cols, dtype=jnp.int32) * block_cols).astype(jnp.int32)
    blocks = lax.map(temporal_block, starts)
    temporal_out = jnp.transpose(blocks, (1, 0, 2, 3, 4)).reshape(FRAMES, SPATIAL, HEADS, HD)
    chosen = (head_class == 1)[None, None, :, None]
    mixed = jnp.where(chosen, temporal_out, spatial_out)
    flat = mixed.reshape(TOKENS, cols)
    return jnp.dot(flat, out_weight, preferred_element_type=jnp.float32).astype(jnp.bfloat16)
```

```python
import functools
import math

import jax
import jax.numpy as jnp
from jax import lax
from jax.experimental import pallas as pl
from jax.experimental.pallas import tpu as pltpu
from jax.sharding import Mesh, PartitionSpec as P

HD = 128
TMAX = 3
FRAMES = 8
TOK = 128
LOCAL = 5
COLS = LOCAL * HD
SCALE = 1.0 / math.sqrt(HD)
TOKEN_AXES = ("frame", "half", "x", "core")
VMEM = pl.BlockSpec(memory_space=pltpu.VMEM)
SMEM = pl.BlockSpec(memory_space=pltpu.SMEM)
PARAMS = pltpu.CompilerParams(vmem_limit_bytes=32 * 1024 * 1024)


def columns(head):
    return pl.ds(pl.multiple_of(head * HD, HD), HD)


def pack_kernel(slots_ref, q_ref, k_ref, v_ref, out_ref):
    for slot in range(TMAX):
        cols = columns(slots_ref[slot])
        for part, source in enumerate((q_ref, k_ref, v_ref)):
            first = (part * TMAX + slot) * HD
            out_ref[:, first : first + HD] = source[:, cols]


def attend(query, key, value, same):
    scores = lax.dot_general(
        query, key, (((1,), (1,)), ((), ())), preferred_element_type=jnp.float32
    )
    scores = jnp.where(same, scores * SCALE, -1e30)
    weights = jnp.exp(scores - jnp.max(scores, axis=-1, keepdims=True))
    weights = weights / jnp.sum(weights, axis=-1, keepdims=True)
    return jnp.dot(
        weights.astype(jnp.bfloat16), value, preferred_element_type=jnp.float32
    ).astype(jnp.bfloat16)


def window_kernel(lengths_ref, q_ref, k_ref, v_ref, out_ref):
    rows = lax.broadcasted_iota(jnp.int32, (TOK, TOK), 0)
    cols = lax.broadcasted_iota(jnp.int32, (TOK, TOK), 1)
    row_id = jnp.zeros((TOK, TOK), jnp.int32)
    col_id = jnp.zeros((TOK, TOK), jnp.int32)
    end = 0
    for window in range(4):
        end = end + lengths_ref[0, window]
        row_id = row_id + (rows >= end).astype(jnp.int32)
        col_id = col_id + (cols >= end).astype(jnp.int32)
    same = row_id == col_id
    for head in range(LOCAL):
        span = slice(head * HD, (head + 1) * HD)
        out_ref[:, span] = attend(q_ref[:, span], k_ref[:, span], v_ref[:, span], same)


def frame_kernel(packed_ref, out_ref):
    width = TOK // FRAMES
    rows = lax.broadcasted_iota(jnp.int32, (TOK, TOK), 0)
    cols = lax.broadcasted_iota(jnp.int32, (TOK, TOK), 1)
    same = (rows & (width - 1)) == (cols & (width - 1))
    for slot in range(TMAX):
        span = [
            slice((part * TMAX + slot) * HD, (part * TMAX + slot + 1) * HD) for part in range(3)
        ]
        out_ref[:, slot * HD : (slot + 1) * HD] = attend(
            packed_ref[:, span[0]], packed_ref[:, span[1]], packed_ref[:, span[2]], same
        )


def mix_kernel(rank_ref, spatial_ref, temporal_ref, out_ref):
    for head in range(LOCAL):
        span = slice(head * HD, (head + 1) * HD)
        rank = rank_ref[head]

        @pl.when(rank < 0)
        def _():
            for copy in range(4):
                out_ref[copy, :, span] = spatial_ref[:, span]

        @pl.when(rank >= 0)
        def _():
            for copy in range(4):
                out_ref[copy, :, span] = temporal_ref[:, columns(jnp.maximum(rank, 0))]


def spread_kernel(weight_ref, out_ref):
    for x in range(4):
        for core in range(2):
            out_ref[2 * x + core] = weight_ref[:, core * COLS : (core + 1) * COLS]


def project_kernel(own_ref, other_ref, weight_ref, out_ref):
    for place, source in enumerate((own_ref, other_ref)):
        total = jnp.zeros((TOK, COLS), jnp.float32)
        for group in range(4):
            total = total + jnp.dot(
                source[group],
                weight_ref[group * COLS : (group + 1) * COLS, :],
                preferred_element_type=jnp.float32,
            )
        out_ref[place] = total.astype(jnp.bfloat16)


def join_kernel(core_ref, both_ref, arrived_ref, out_ref):
    core = core_ref[0]
    out_ref[:, pl.ds(pl.multiple_of(core * COLS, HD), COLS)] = both_ref[0]
    out_ref[:, pl.ds(pl.multiple_of((1 - core) * COLS, HD), COLS)] = arrived_ref[...]


def call(kernel, out_shape, specs, *args, scratch=(), flops=0):
    size = sum(a.size * a.dtype.itemsize for a in args) + math.prod(out_shape) * 2
    return pl.pallas_call(
        kernel,
        out_shape=jax.ShapeDtypeStruct(out_shape, jnp.bfloat16),
        in_specs=specs,
        out_specs=VMEM,
        scratch_shapes=scratch,
        compiler_params=PARAMS,
        cost_estimate=pl.CostEstimate(flops=flops, bytes_accessed=size, transcendentals=0),
    )(*args)


def body(queries, keys, values, head_class, window_lengths, out_weight):
    core = lax.axis_index("core")
    group = lax.axis_index("head")
    classes = lax.dynamic_slice_in_dim(head_class, group * LOCAL, LOCAL)
    temporal = classes == 1
    rank = jnp.where(temporal, jnp.cumsum(temporal.astype(jnp.int32)) - 1, -1)
    slots = jnp.sum(
        jnp.where(
            rank[None, :] == jnp.arange(TMAX, dtype=jnp.int32)[:, None],
            jnp.arange(LOCAL, dtype=jnp.int32)[None, :],
            0,
        ),
        axis=1,
    ).astype(jnp.int32)

    weight = call(spread_kernel, (8, 20, COLS), [VMEM], out_weight)
    weight = lax.all_to_all(weight, ("x", "core"), 0, 0, tiled=True).reshape(160, COLS)

    width = TOK // FRAMES
    packed = call(
        pack_kernel, (TOK, 3 * TMAX * HD), [SMEM] + [VMEM] * 3, slots, queries, keys, values
    )
    packed, weight = lax.optimization_barrier((packed, weight))
    weight = lax.all_gather(weight, ("frame", "half"), axis=0, tiled=True)
    packed = lax.all_to_all(
        packed.reshape(FRAMES, width, 3 * TMAX * HD), "frame", 0, 0, tiled=True
    ).reshape(TOK, 3 * TMAX * HD)
    spatial = call(
        window_kernel, (TOK, COLS), [SMEM] + [VMEM] * 3, window_lengths, queries, keys, values
    )
    attended = call(frame_kernel, (TOK, TMAX * HD), [VMEM], packed)
    attended = lax.all_to_all(
        attended.reshape(FRAMES, width, TMAX * HD), "frame", 0, 0, tiled=True
    ).reshape(TOK, TMAX * HD)

    mixed = call(
        mix_kernel, (4, TOK, COLS), [SMEM] + [VMEM] * 2, rank, spatial, attended
    )
    mixed = lax.all_to_all(mixed, "head", 0, 0, tiled=True)
    swap = [(0, 1), (1, 0)]
    other = lax.ppermute(mixed, "core", swap)
    both = call(
        project_kernel,
        (2, TOK, COLS),
        [VMEM] * 3,
        mixed,
        other,
        weight,
        flops=2 * TOK * 2560 * 1280,
    )
    arrived = lax.ppermute(both[1], "core", swap)
    return call(
        join_kernel,
        (TOK, 2 * COLS),
        [SMEM] + [VMEM] * 2,
        core.astype(jnp.int32).reshape(1),
        both,
        arrived,
    )


def solution(mesh):
    mesh = Mesh(mesh.devices.reshape(8, 2, 4, 2, 4), TOKEN_AXES + ("head",))
    split = P(TOKEN_AXES, "head")
    placed = (split, split, split, P(), P(TOKEN_AXES, None), split)
    return jax.shard_map(body, mesh=mesh, in_specs=placed, out_specs=split, check_vma=False)
```

```python
import functools
import math

import jax
import jax.numpy as jnp
from jax import lax
from jax.experimental import pallas as pl
from jax.experimental.pallas import tpu as pltpu
from jax.sharding import Mesh, PartitionSpec as P

HD = 128
TMAX = 3
FRAMES = 8
TOK = 128
LOCAL = 5
COLS = LOCAL * HD
PART = 384
SCALE = 1.0 / math.sqrt(HD)
TOKEN_AXES = ("frame", "half", "x", "core")
VMEM = pl.BlockSpec(memory_space=pltpu.VMEM)
SMEM = pl.BlockSpec(memory_space=pltpu.SMEM)
HBM = pl.BlockSpec(memory_space=pltpu.HBM)
PARAMS = pltpu.CompilerParams(vmem_limit_bytes=16 * 1024 * 1024)


def columns(head):
    return pl.ds(pl.multiple_of(head * HD, HD), HD)


def ranks(classes_ref, group):
    found, before = [], 0
    for head in range(LOCAL):
        temporal = classes_ref[group * LOCAL + head] == 1
        found.append((temporal, before))
        before = before + temporal.astype(jnp.int32)
    return found


def pack_kernel(group_ref, classes_ref, q_ref, k_ref, v_ref, out_ref, sems):
    slots = [0] * TMAX
    for head, (temporal, before) in enumerate(ranks(classes_ref, group_ref[0])):
        slots = [
            jnp.where(temporal & (before == slot), head, taken)
            for slot, taken in enumerate(slots)
        ]
    copies = []
    for part, source in enumerate((q_ref, k_ref, v_ref)):
        for slot in range(TMAX):
            place = part * TMAX + slot
            copies.append(
                pltpu.make_async_copy(
                    source.at[:, columns(slots[slot])],
                    out_ref.at[:, place * HD : (place + 1) * HD],
                    sems.at[place],
                )
            )
    for copy in copies:
        copy.start()
    for copy in copies:
        copy.wait()


def attend(query, key, value, same):
    scores = lax.dot_general(
        query, key, (((1,), (1,)), ((), ())), preferred_element_type=jnp.float32
    )
    scores = jnp.where(same, scores * SCALE, -1e30)
    weights = jnp.exp(scores - jnp.max(scores, axis=-1, keepdims=True))
    weights = weights / jnp.sum(weights, axis=-1, keepdims=True)
    return jnp.dot(
        weights.astype(jnp.bfloat16), value, preferred_element_type=jnp.float32
    ).astype(jnp.bfloat16)


def window_kernel(lengths_ref, q_ref, k_ref, v_ref, out_ref):
    rows = lax.broadcasted_iota(jnp.int32, (TOK, TOK), 0)
    cols = lax.broadcasted_iota(jnp.int32, (TOK, TOK), 1)
    row_id = jnp.zeros((TOK, TOK), jnp.int32)
    col_id = jnp.zeros((TOK, TOK), jnp.int32)
    end = 0
    for window in range(4):
        end = end + lengths_ref[0, window]
        row_id = row_id + (rows >= end).astype(jnp.int32)
        col_id = col_id + (cols >= end).astype(jnp.int32)
    same = row_id == col_id
    for head in range(LOCAL):
        span = slice(head * HD, (head + 1) * HD)
        out_ref[:, span] = attend(q_ref[:, span], k_ref[:, span], v_ref[:, span], same)


def frame_kernel(packed_ref, out_ref):
    width = TOK // FRAMES
    rows = lax.broadcasted_iota(jnp.int32, (TOK, TOK), 0)
    cols = lax.broadcasted_iota(jnp.int32, (TOK, TOK), 1)
    same = (rows & (width - 1)) == (cols & (width - 1))
    for slot in range(TMAX):
        span = [
            slice((part * TMAX + slot) * HD, (part * TMAX + slot + 1) * HD) for part in range(3)
        ]
        out_ref[:, slot * HD : (slot + 1) * HD] = attend(
            packed_ref[:, span[0]], packed_ref[:, span[1]], packed_ref[:, span[2]], same
        )


def mix_kernel(group_ref, classes_ref, spatial_ref, temporal_ref, order_ref, out_ref, mixed):
    for head, (temporal, before) in enumerate(ranks(classes_ref, group_ref[0])):
        span = slice(head * HD, (head + 1) * HD)

        @pl.when(jnp.logical_not(temporal))
        def _():
            mixed[:, span] = spatial_ref[:, span]

        @pl.when(temporal)
        def _():
            mixed[:, span] = temporal_ref[:, columns(before)]

    ordered = jnp.dot(mixed[...], order_ref[...], preferred_element_type=jnp.float32)
    ordered = ordered.astype(jnp.bfloat16)
    for copy in range(4):
        for core in range(2):
            out_ref[2 * copy + core] = ordered[:, core * PART : (core + 1) * PART]


def rows_kernel(weight_ref, out_ref):
    for group in range(4):
        out_ref[group * 80 : (group + 1) * 80, :] = jnp.concatenate(
            [weight_ref[4 * group + z] for z in range(4)], axis=0
        )


def project_kernel(core_ref, mixed_ref, w0_ref, w1_ref, w2_ref, w3_ref, own_ref, other_ref):
    core = core_ref[0]
    zeros = jnp.zeros((PART - 320, 2 * COLS), jnp.bfloat16)
    total = jnp.zeros((2 * TOK, 2 * COLS), jnp.float32)
    for group in range(4):
        span = slice(group * 80, (group + 1) * 80)
        rows = [w[span, :] for w in (w0_ref, w1_ref, w2_ref, w3_ref)]
        tokens = jnp.concatenate(
            [mixed_ref[2 * group + core], mixed_ref[2 * group + 1 - core]], axis=0
        )
        total = total + jnp.dot(
            tokens,
            jnp.concatenate(rows + [zeros], axis=0),
            preferred_element_type=jnp.float32,
        )
    own_ref[...] = total[:TOK]
    other_ref[...] = total[TOK:]


def sum_kernel(own_ref, arrived_ref, out_ref):
    out_ref[...] = (own_ref[...] + arrived_ref[...]).astype(jnp.bfloat16)


def call(kernel, out_shape, specs, *args, scratch=(), flops=0, out_dtype=jnp.bfloat16):
    shapes = out_shape if isinstance(out_shape, list) else [out_shape]
    size = sum(a.size * a.dtype.itemsize for a in args)
    size += sum(math.prod(shape) * jnp.dtype(out_dtype).itemsize for shape in shapes)
    results = pl.pallas_call(
        kernel,
        out_shape=[jax.ShapeDtypeStruct(shape, out_dtype) for shape in shapes],
        in_specs=specs,
        out_specs=[VMEM] * len(shapes),
        scratch_shapes=scratch,
        compiler_params=PARAMS,
        cost_estimate=pl.CostEstimate(flops=flops, bytes_accessed=size, transcendentals=0),
    )(*args)
    return results if isinstance(out_shape, list) else results[0]


def body(queries, keys, values, head_class, window_lengths, out_weight):
    core = lax.axis_index("core").astype(jnp.int32).reshape(1)
    group = lax.axis_index("head").astype(jnp.int32).reshape(1)
    width = TOK // FRAMES
    packed = call(
        pack_kernel,
        (TOK, 3 * TMAX * HD),
        [SMEM] * 2 + [HBM] * 3,
        group,
        head_class,
        queries,
        keys,
        values,
        scratch=[pltpu.SemaphoreType.DMA((3 * TMAX,))],
    )
    packed, weight = lax.optimization_barrier((packed, out_weight))
    weight = lax.all_gather(weight, ("frame", "half"), axis=0, tiled=False)
    packed = lax.all_to_all(
        packed.reshape(FRAMES, width, 3 * TMAX * HD), "frame", 0, 0, tiled=True
    ).reshape(TOK, 3 * TMAX * HD)
    packed, weight = lax.optimization_barrier((packed, weight))
    attended = call(frame_kernel, (TOK, TMAX * HD), [VMEM], packed)
    attended, weight, queries, keys, values = lax.optimization_barrier(
        (attended, weight, queries, keys, values)
    )
    weight = call(rows_kernel, (320, 2 * COLS), [VMEM], weight)
    around = [
        lax.ppermute(weight, "x", [((x + step) % 4, x) for x in range(4)]) for step in (1, 2, 3)
    ]
    spatial = call(
        window_kernel, (TOK, COLS), [SMEM] + [VMEM] * 3, window_lengths, queries, keys, values
    )
    attended = lax.all_to_all(
        attended.reshape(FRAMES, width, TMAX * HD), "frame", 0, 0, tiled=True
    ).reshape(TOK, TMAX * HD)

    source = jnp.arange(COLS, dtype=jnp.int32)[:, None]
    place = jnp.arange(2 * PART, dtype=jnp.int32)[None, :]
    rest = place % PART
    owner = (lax.axis_index("x") + rest // 80) % 4
    wanted = rest % 80 // 20 * 160 + owner * 40 + place // PART * 20 + rest % 20
    order = ((source == wanted) & (rest < 320)).astype(jnp.bfloat16)
    mixed = call(
        mix_kernel,
        (8, TOK, PART),
        [SMEM] * 2 + [VMEM] * 3,
        group,
        head_class,
        spatial,
        attended,
        order,
        scratch=[pltpu.VMEM((TOK, COLS), jnp.bfloat16)],
    )
    mixed = lax.all_to_all(mixed, ("head", "core"), 0, 0, tiled=True)
    own, other = call(
        project_kernel,
        [(TOK, 2 * COLS)] * 2,
        [SMEM] + [VMEM] * 5,
        core,
        mixed,
        weight,
        *around,
        flops=2 * TOK * 2560 * 1280,
        out_dtype=jnp.float32,
    )
    arrived = lax.ppermute(other, "core", [(0, 1), (1, 0)])
    return call(sum_kernel, (TOK, 2 * COLS), [VMEM] * 2, own, arrived)


def solution(mesh):
    mesh = Mesh(mesh.devices.reshape(8, 2, 4, 2, 4), TOKEN_AXES + ("head",))
    split = P(TOKEN_AXES, "head")
    placed = (split, split, split, P(), P(TOKEN_AXES, None), split)
    return jax.shard_map(body, mesh=mesh, in_specs=placed, out_specs=split, check_vma=False)
```

```python
import functools
import math

import jax
import jax.numpy as jnp
from jax import lax
from jax.experimental import pallas as pl
from jax.experimental.pallas import tpu as pltpu
from jax.sharding import Mesh, PartitionSpec as P

HD = 128
TMAX = 3
FRAMES = 8
TOK = 128
LOCAL = 5
COLS = LOCAL * HD
SCALE = 1.0 / math.sqrt(HD)
FRAME_AXES = ("far", "near")
Z_AXES = ("far", "near", "half")
TOKEN_AXES = Z_AXES + ("x", "core")
VMEM = pl.BlockSpec(memory_space=pltpu.VMEM)
SMEM = pl.BlockSpec(memory_space=pltpu.SMEM)
HBM = pl.BlockSpec(memory_space=pltpu.HBM)


def columns(head):
    return pl.ds(pl.multiple_of(head * HD, HD), HD)


def ranks(classes_ref, group):
    found, before = [], 0
    for head in range(LOCAL):
        temporal = classes_ref[group * LOCAL + head] == 1
        found.append((temporal, before))
        before = before + temporal.astype(jnp.int32)
    return found


def pack_kernel(group_ref, classes_ref, q_ref, k_ref, v_ref, out_ref, sems):
    slots = [0] * TMAX
    for head, (temporal, before) in enumerate(ranks(classes_ref, group_ref[0])):
        slots = [
            jnp.where(temporal & (before == slot), head, taken)
            for slot, taken in enumerate(slots)
        ]
    copies = []
    for part, source in enumerate((q_ref, k_ref, v_ref)):
        for slot in range(TMAX):
            place = part * TMAX + slot
            copies.append(
                pltpu.make_async_copy(
                    source.at[:, columns(slots[slot])],
                    out_ref.at[:, place * HD : (place + 1) * HD],
                    sems.at[place],
                )
            )
    for copy in copies:
        copy.start()
    for copy in copies:
        copy.wait()


def attend(query, key, value, same):
    scores = lax.dot_general(
        query, key, (((1,), (1,)), ((), ())), preferred_element_type=jnp.float32
    )
    scores = jnp.where(same, scores * SCALE, -1e30)
    weights = jnp.exp(scores - jnp.max(scores, axis=-1, keepdims=True))
    weights = weights / jnp.sum(weights, axis=-1, keepdims=True)
    return jnp.dot(
        weights.astype(jnp.bfloat16), value, preferred_element_type=jnp.float32
    ).astype(jnp.bfloat16)


def window_kernel(lengths_ref, q_hbm, k_hbm, v_hbm, out_ref, q_ref, k_ref, v_ref, sems):
    copies = [
        pltpu.make_async_copy(source, target, sems.at[place])
        for place, (source, target) in enumerate(
            ((q_hbm, q_ref), (k_hbm, k_ref), (v_hbm, v_ref))
        )
    ]
    for copy in copies:
        copy.start()
    for copy in copies:
        copy.wait()
    rows = lax.broadcasted_iota(jnp.int32, (TOK, TOK), 0)
    cols = lax.broadcasted_iota(jnp.int32, (TOK, TOK), 1)
    row_id = jnp.zeros((TOK, TOK), jnp.int32)
    col_id = jnp.zeros((TOK, TOK), jnp.int32)
    end = 0
    for window in range(4):
        end = end + lengths_ref[0, window]
        row_id = row_id + (rows >= end).astype(jnp.int32)
        col_id = col_id + (cols >= end).astype(jnp.int32)
    same = row_id == col_id
    for head in range(LOCAL):
        span = slice(head * HD, (head + 1) * HD)
        out_ref[:, span] = attend(q_ref[:, span], k_ref[:, span], v_ref[:, span], same)


def frame_kernel(packed_ref, out_ref, mark_ref):
    width = TOK // FRAMES
    rows = lax.broadcasted_iota(jnp.int32, (TOK, TOK), 0)
    cols = lax.broadcasted_iota(jnp.int32, (TOK, TOK), 1)
    same = (rows & (width - 1)) == (cols & (width - 1))
    mark_ref[...] = packed_ref[:16, :HD]
    for slot in range(TMAX):
        span = [
            slice((part * TMAX + slot) * HD, (part * TMAX + slot + 1) * HD) for part in range(3)
        ]
        out_ref[:, slot * HD : (slot + 1) * HD] = attend(
            packed_ref[:, span[0]], packed_ref[:, span[1]], packed_ref[:, span[2]], same
        )


def mix_kernel(group_ref, classes_ref, spatial_ref, temporal_ref, order_ref, out_ref, mixed):
    for head, (temporal, before) in enumerate(ranks(classes_ref, group_ref[0])):
        span = slice(head * HD, (head + 1) * HD)

        @pl.when(jnp.logical_not(temporal))
        def _():
            mixed[:, span] = spatial_ref[:, span]

        @pl.when(temporal)
        def _():
            mixed[:, span] = temporal_ref[:, columns(before)]

    ordered = jnp.dot(mixed[...], order_ref[...], preferred_element_type=jnp.float32)
    ordered = ordered.astype(jnp.bfloat16)
    for copy in range(4):
        out_ref[copy] = ordered


def rows_kernel(weight_ref, out_ref):
    for group in range(4):
        out_ref[group * 80 : (group + 1) * 80, :] = jnp.concatenate(
            [weight_ref[4 * group + z] for z in range(4)], axis=0
        )


def project_kernel(mixed_ref, mark_ref, *refs):
    slabs, out_ref = refs[:8], refs[8]
    total = jnp.zeros((TOK, 2 * COLS), jnp.float32)
    for group in range(4):
        rows = [slab[group * 80 : (group + 1) * 80, :] for slab in slabs]
        total = total + jnp.dot(
            mixed_ref[group],
            jnp.concatenate(rows, axis=0),
            preferred_element_type=jnp.float32,
        )
    out_ref[...] = total.astype(jnp.bfloat16)


def call(kernel, out_shape, specs, *args, scratch=(), flops=0, out_dtype=jnp.bfloat16, vmem=16):
    shapes = out_shape if isinstance(out_shape, list) else [out_shape]
    size = sum(a.size * a.dtype.itemsize for a in args)
    size += sum(math.prod(shape) * jnp.dtype(out_dtype).itemsize for shape in shapes)
    results = pl.pallas_call(
        kernel,
        out_shape=[jax.ShapeDtypeStruct(shape, out_dtype) for shape in shapes],
        in_specs=specs,
        out_specs=[VMEM] * len(shapes),
        scratch_shapes=scratch,
        compiler_params=pltpu.CompilerParams(vmem_limit_bytes=vmem << 20),
        cost_estimate=pl.CostEstimate(flops=flops, bytes_accessed=size, transcendentals=0),
    )(*args)
    return results if isinstance(out_shape, list) else results[0]


def body(queries, keys, values, head_class, window_lengths, out_weight):
    core = lax.axis_index("core")
    group = lax.axis_index("head").astype(jnp.int32).reshape(1)
    width = TOK // FRAMES
    packed = call(
        pack_kernel,
        (TOK, 3 * TMAX * HD),
        [SMEM] * 2 + [HBM] * 3,
        group,
        head_class,
        queries,
        keys,
        values,
        scratch=[pltpu.SemaphoreType.DMA((3 * TMAX,))],
        vmem=60,
    )
    weight = lax.all_gather(out_weight, Z_AXES, axis=0, tiled=False)
    packed, weight = lax.optimization_barrier((packed, weight))
    packed = lax.all_to_all(
        packed.reshape(FRAMES, width, 3 * TMAX * HD), FRAME_AXES, 0, 0, tiled=True
    ).reshape(TOK, 3 * TMAX * HD)
    weight = call(rows_kernel, (320, 2 * COLS), [VMEM], weight)
    around = [
        lax.ppermute(weight, "x", [((x + step) % 4, x) for x in range(4)]) for step in (1, 2, 3)
    ]
    attended, mark = call(frame_kernel, [(TOK, TMAX * HD), (16, HD)], [VMEM], packed)
    spatial = call(
        window_kernel,
        (TOK, COLS),
        [SMEM] + [HBM] * 3,
        window_lengths,
        queries,
        keys,
        values,
        scratch=[pltpu.VMEM((TOK, COLS), jnp.bfloat16)] * 3 + [pltpu.SemaphoreType.DMA((3,))],
    )
    mark, weight, around = lax.optimization_barrier((mark, weight, around))
    swap = [(0, 1), (1, 0)]
    slabs = [weight, *around]
    slabs = slabs + [lax.ppermute(slab, "core", swap) for slab in slabs]
    attended = lax.all_to_all(
        attended.reshape(FRAMES, width, TMAX * HD), FRAME_AXES, 0, 0, tiled=True
    ).reshape(TOK, TMAX * HD)

    source = jnp.arange(COLS, dtype=jnp.int32)[:, None]
    place = jnp.arange(COLS, dtype=jnp.int32)[None, :]
    owner = (lax.axis_index("x") + place // 80) % 4 * 2 + (core + place // 320) % 2
    wanted = place % 80 // 20 * 160 + owner * 20 + place % 20
    order = (source == wanted).astype(jnp.bfloat16)
    mixed = call(
        mix_kernel,
        (4, TOK, COLS),
        [SMEM] * 2 + [VMEM] * 3,
        group,
        head_class,
        spatial,
        attended,
        order,
        scratch=[pltpu.VMEM((TOK, COLS), jnp.bfloat16)],
    )
    mixed = lax.all_to_all(mixed, "head", 0, 0, tiled=True)
    return call(
        project_kernel,
        (TOK, 2 * COLS),
        [VMEM] * 10,
        mixed,
        mark,
        *slabs,
        flops=2 * TOK * 2560 * 1280,
    )


def solution(mesh):
    mesh = Mesh(mesh.devices.reshape(4, 2, 2, 4, 2, 4), TOKEN_AXES + ("head",))
    split = P(TOKEN_AXES, "head")
    placed = (split, split, split, P(), P(TOKEN_AXES, None), split)
    return jax.shard_map(body, mesh=mesh, in_specs=placed, out_specs=split, check_vma=False)
```

```python
import functools
import math

import jax
import jax.numpy as jnp
from jax import lax
from jax.experimental import pallas as pl
from jax.experimental.pallas import tpu as pltpu
from jax.sharding import Mesh, PartitionSpec as P

HD = 128
TMAX = 3
FRAMES = 8
TOK = 128
LOCAL = 5
COLS = LOCAL * HD
SCALE = 1.0 / math.sqrt(HD)
FRAME_AXES = ("far", "near")
Z_AXES = ("far", "near", "half")
TOKEN_AXES = Z_AXES + ("x", "core")
VMEM = pl.BlockSpec(memory_space=pltpu.VMEM)
SMEM = pl.BlockSpec(memory_space=pltpu.SMEM)
HBM = pl.BlockSpec(memory_space=pltpu.HBM)


def columns(head):
    return pl.ds(pl.multiple_of(head * HD, HD), HD)


def ranks(classes_ref, group):
    found, before = [], 0
    for head in range(LOCAL):
        temporal = classes_ref[group * LOCAL + head] == 1
        found.append((temporal, before))
        before = before + temporal.astype(jnp.int32)
    return found


def pack_kernel(group_ref, classes_ref, q_ref, k_ref, v_ref, out_ref, sems):
    slots = [0] * TMAX
    for head, (temporal, before) in enumerate(ranks(classes_ref, group_ref[0])):
        slots = [
            jnp.where(temporal & (before == slot), head, taken)
            for slot, taken in enumerate(slots)
        ]
    copies = []
    for part, source in enumerate((q_ref, k_ref, v_ref)):
        for slot in range(TMAX):
            place = part * TMAX + slot
            copies.append(
                pltpu.make_async_copy(
                    source.at[:, columns(slots[slot])],
                    out_ref.at[:, place * HD : (place + 1) * HD],
                    sems.at[place],
                )
            )
    for copy in copies:
        copy.start()
    for copy in copies:
        copy.wait()


def attend(query, key, value, same):
    scores = lax.dot_general(
        query, key, (((1,), (1,)), ((), ())), preferred_element_type=jnp.float32
    )
    scores = jnp.where(same, scores * SCALE, -1e30)
    weights = jnp.exp(scores - jnp.max(scores, axis=-1, keepdims=True))
    weights = weights / jnp.sum(weights, axis=-1, keepdims=True)
    return jnp.dot(
        weights.astype(jnp.bfloat16), value, preferred_element_type=jnp.float32
    ).astype(jnp.bfloat16)


def window_kernel(lengths_ref, q_hbm, k_hbm, v_hbm, out_ref, q_ref, k_ref, v_ref, sems):
    copies = [
        pltpu.make_async_copy(source, target, sems.at[place])
        for place, (source, target) in enumerate(
            ((q_hbm, q_ref), (k_hbm, k_ref), (v_hbm, v_ref))
        )
    ]
    for copy in copies:
        copy.start()
    for copy in copies:
        copy.wait()
    rows = lax.broadcasted_iota(jnp.int32, (TOK, TOK), 0)
    cols = lax.broadcasted_iota(jnp.int32, (TOK, TOK), 1)
    row_id = jnp.zeros((TOK, TOK), jnp.int32)
    col_id = jnp.zeros((TOK, TOK), jnp.int32)
    end = 0
    for window in range(4):
        end = end + lengths_ref[0, window]
        row_id = row_id + (rows >= end).astype(jnp.int32)
        col_id = col_id + (cols >= end).astype(jnp.int32)
    same = row_id == col_id
    for head in range(LOCAL):
        span = slice(head * HD, (head + 1) * HD)
        out_ref[:, span] = attend(q_ref[:, span], k_ref[:, span], v_ref[:, span], same)


def frame_kernel(packed_ref, out_ref, mark_ref):
    width = TOK // FRAMES
    rows = lax.broadcasted_iota(jnp.int32, (TOK, TOK), 0)
    cols = lax.broadcasted_iota(jnp.int32, (TOK, TOK), 1)
    same = (rows & (width - 1)) == (cols & (width - 1))
    mark_ref[...] = packed_ref[:16, :HD]
    for slot in range(TMAX):
        span = [
            slice((part * TMAX + slot) * HD, (part * TMAX + slot + 1) * HD) for part in range(3)
        ]
        out_ref[:, slot * HD : (slot + 1) * HD] = attend(
            packed_ref[:, span[0]], packed_ref[:, span[1]], packed_ref[:, span[2]], same
        )


def mix_kernel(group_ref, classes_ref, spatial_ref, temporal_ref, order_ref, out_ref, mixed):
    for head, (temporal, before) in enumerate(ranks(classes_ref, group_ref[0])):
        span = slice(head * HD, (head + 1) * HD)

        @pl.when(jnp.logical_not(temporal))
        def _():
            mixed[:, span] = spatial_ref[:, span]

        @pl.when(temporal)
        def _():
            mixed[:, span] = temporal_ref[:, columns(before)]

    ordered = jnp.dot(mixed[...], order_ref[...], preferred_element_type=jnp.float32)
    ordered = ordered.astype(jnp.bfloat16)
    for copy in range(4):
        out_ref[copy] = ordered


def rows_kernel(weight_ref, out_ref):
    for group in range(4):
        out_ref[group * 80 : (group + 1) * 80, :] = jnp.concatenate(
            [weight_ref[4 * group + z] for z in range(4)], axis=0
        )


def project_kernel(mixed_ref, mark_ref, *refs):
    slabs, out_ref = refs[:8], refs[8]
    total = jnp.zeros((TOK, 2 * COLS), jnp.float32)
    for group in range(4):
        rows = [slab[group * 80 : (group + 1) * 80, :] for slab in slabs]
        total = total + jnp.dot(
            mixed_ref[group],
            jnp.concatenate(rows, axis=0),
            preferred_element_type=jnp.float32,
        )
    out_ref[...] = total.astype(jnp.bfloat16)


def call(kernel, out_shape, specs, *args, scratch=(), flops=0, out_dtype=jnp.bfloat16, vmem=16):
    shapes = out_shape if isinstance(out_shape, list) else [out_shape]
    size = sum(a.size * a.dtype.itemsize for a in args)
    size += sum(math.prod(shape) * jnp.dtype(out_dtype).itemsize for shape in shapes)
    results = pl.pallas_call(
        kernel,
        out_shape=[jax.ShapeDtypeStruct(shape, out_dtype) for shape in shapes],
        in_specs=specs,
        out_specs=[VMEM] * len(shapes),
        scratch_shapes=scratch,
        compiler_params=pltpu.CompilerParams(vmem_limit_bytes=vmem << 20),
        cost_estimate=pl.CostEstimate(flops=flops, bytes_accessed=size, transcendentals=0),
    )(*args)
    return results if isinstance(out_shape, list) else results[0]


def body(queries, keys, values, head_class, window_lengths, out_weight):
    core = lax.axis_index("core")
    group = lax.axis_index("head").astype(jnp.int32).reshape(1)
    width = TOK // FRAMES
    weight = lax.all_gather(out_weight, Z_AXES, axis=0, tiled=False)
    weight = call(rows_kernel, (320, 2 * COLS), [VMEM], weight)
    around = [
        lax.ppermute(weight, "x", [((x + step) % 4, x) for x in range(4)]) for step in (1, 2, 3)
    ]
    queries, keys, values, weight = lax.optimization_barrier((queries, keys, values, weight))
    packed = call(
        pack_kernel,
        (TOK, 3 * TMAX * HD),
        [SMEM] * 2 + [HBM] * 3,
        group,
        head_class,
        queries,
        keys,
        values,
        scratch=[pltpu.SemaphoreType.DMA((3 * TMAX,))],
        vmem=60,
    )
    packed = lax.all_to_all(
        packed.reshape(FRAMES, width, 3 * TMAX * HD), FRAME_AXES, 0, 0, tiled=True
    ).reshape(TOK, 3 * TMAX * HD)
    spatial = call(
        window_kernel,
        (TOK, COLS),
        [SMEM] + [HBM] * 3,
        window_lengths,
        queries,
        keys,
        values,
        scratch=[pltpu.VMEM((TOK, COLS), jnp.bfloat16)] * 3 + [pltpu.SemaphoreType.DMA((3,))],
    )
    packed, spatial = lax.optimization_barrier((packed, spatial))
    attended, mark = call(frame_kernel, [(TOK, TMAX * HD), (16, HD)], [VMEM], packed)
    mark, weight = lax.optimization_barrier((mark, weight))
    mark, around = lax.optimization_barrier((mark, around))
    swap = [(0, 1), (1, 0)]
    slabs = [weight, *around]
    slabs = slabs + [lax.ppermute(slab, "core", swap) for slab in slabs]
    attended = lax.all_to_all(
        attended.reshape(FRAMES, width, TMAX * HD), FRAME_AXES, 0, 0, tiled=True
    ).reshape(TOK, TMAX * HD)

    source = jnp.arange(COLS, dtype=jnp.int32)[:, None]
    place = jnp.arange(COLS, dtype=jnp.int32)[None, :]
    owner = (lax.axis_index("x") + place // 80) % 4 * 2 + (core + place // 320) % 2
    wanted = place % 80 // 20 * 160 + owner * 20 + place % 20
    order = (source == wanted).astype(jnp.bfloat16)
    mixed = call(
        mix_kernel,
        (4, TOK, COLS),
        [SMEM] * 2 + [VMEM] * 3,
        group,
        head_class,
        spatial,
        attended,
        order,
        scratch=[pltpu.VMEM((TOK, COLS), jnp.bfloat16)],
    )
    mixed = lax.all_to_all(mixed, "head", 0, 0, tiled=True)
    return call(
        project_kernel,
        (TOK, 2 * COLS),
        [VMEM] * 10,
        mixed,
        mark,
        *slabs,
        flops=2 * TOK * 2560 * 1280,
    )


def solution(mesh):
    mesh = Mesh(mesh.devices.reshape(4, 2, 2, 4, 2, 4), TOKEN_AXES + ("head",))
    split = P(TOKEN_AXES, "head")
    placed = (split, split, split, P(), P(TOKEN_AXES, None), split)
    return jax.shard_map(body, mesh=mesh, in_specs=placed, out_specs=split, check_vma=False)
```

```python
import functools
import math

import jax
import jax.numpy as jnp
from jax import lax
from jax.experimental import pallas as pl
from jax.experimental.pallas import tpu as pltpu
from jax.sharding import Mesh, PartitionSpec as P

HD = 128
TMAX = 3
FRAMES = 8
TOK = 128
LOCAL = 5
COLS = LOCAL * HD
SCALE = 1.0 / math.sqrt(HD)
FRAME_AXES = ("far", "near")
Z_AXES = ("far", "near", "half")
TOKEN_AXES = Z_AXES + ("x", "core")
VMEM = pl.BlockSpec(memory_space=pltpu.VMEM)
SMEM = pl.BlockSpec(memory_space=pltpu.SMEM)
HBM = pl.BlockSpec(memory_space=pltpu.HBM)


def columns(head):
    return pl.ds(pl.multiple_of(head * HD, HD), HD)


def ranks(classes_ref, group):
    found, before = [], 0
    for head in range(LOCAL):
        temporal = classes_ref[group * LOCAL + head] == 1
        found.append((temporal, before))
        before = before + temporal.astype(jnp.int32)
    return found


def pack_kernel(group_ref, classes_ref, q_ref, k_ref, v_ref, out_ref):
    slots = [0] * TMAX
    for head, (temporal, before) in enumerate(ranks(classes_ref, group_ref[0])):
        slots = [
            jnp.where(temporal & (before == slot), head, taken)
            for slot, taken in enumerate(slots)
        ]
    for part, source in enumerate((q_ref, k_ref, v_ref)):
        for slot in range(TMAX):
            place = (part * TMAX + slot) * HD
            out_ref[:, place : place + HD] = source[:, columns(slots[slot])]


def attend(query, key, value, same):
    scores = lax.dot_general(
        query, key, (((1,), (1,)), ((), ())), preferred_element_type=jnp.float32
    )
    scores = jnp.where(same, scores * SCALE, -1e30)
    weights = jnp.exp(scores - jnp.max(scores, axis=-1, keepdims=True))
    weights = weights / jnp.sum(weights, axis=-1, keepdims=True)
    return jnp.dot(
        weights.astype(jnp.bfloat16), value, preferred_element_type=jnp.float32
    ).astype(jnp.bfloat16)


def window_kernel(lengths_ref, q_ref, k_ref, v_ref, out_ref):
    rows = lax.broadcasted_iota(jnp.int32, (TOK, TOK), 0)
    cols = lax.broadcasted_iota(jnp.int32, (TOK, TOK), 1)
    row_id = jnp.zeros((TOK, TOK), jnp.int32)
    col_id = jnp.zeros((TOK, TOK), jnp.int32)
    end = 0
    for window in range(4):
        end = end + lengths_ref[0, window]
        row_id = row_id + (rows >= end).astype(jnp.int32)
        col_id = col_id + (cols >= end).astype(jnp.int32)
    same = row_id == col_id
    for head in range(LOCAL):
        span = slice(head * HD, (head + 1) * HD)
        out_ref[:, span] = attend(q_ref[:, span], k_ref[:, span], v_ref[:, span], same)


def frame_kernel(packed_ref, out_ref, mark_ref):
    width = TOK // FRAMES
    rows = lax.broadcasted_iota(jnp.int32, (TOK, TOK), 0)
    cols = lax.broadcasted_iota(jnp.int32, (TOK, TOK), 1)
    same = (rows & (width - 1)) == (cols & (width - 1))
    mark_ref[...] = packed_ref[:16, :HD]
    for slot in range(TMAX):
        span = [
            slice((part * TMAX + slot) * HD, (part * TMAX + slot + 1) * HD) for part in range(3)
        ]
        out_ref[:, slot * HD : (slot + 1) * HD] = attend(
            packed_ref[:, span[0]], packed_ref[:, span[1]], packed_ref[:, span[2]], same
        )


def mix_kernel(group_ref, classes_ref, spatial_ref, temporal_ref, order_ref, out_ref, mixed):
    for head, (temporal, before) in enumerate(ranks(classes_ref, group_ref[0])):
        span = slice(head * HD, (head + 1) * HD)

        @pl.when(jnp.logical_not(temporal))
        def _():
            mixed[:, span] = spatial_ref[:, span]

        @pl.when(temporal)
        def _():
            mixed[:, span] = temporal_ref[:, columns(before)]

    ordered = jnp.dot(mixed[...], order_ref[...], preferred_element_type=jnp.float32)
    ordered = ordered.astype(jnp.bfloat16)
    for copy in range(4):
        out_ref[copy] = ordered


def rows_kernel(weight_ref, out_ref):
    for group in range(4):
        out_ref[group * 80 : (group + 1) * 80, :] = jnp.concatenate(
            [weight_ref[4 * group + z] for z in range(4)], axis=0
        )


def project_kernel(mixed_ref, mark_ref, *refs):
    slabs, out_ref = refs[:8], refs[8]
    total = jnp.zeros((TOK, 2 * COLS), jnp.float32)
    for group in range(4):
        rows = [slab[group * 80 : (group + 1) * 80, :] for slab in slabs]
        total = total + jnp.dot(
            mixed_ref[group],
            jnp.concatenate(rows, axis=0),
            preferred_element_type=jnp.float32,
        )
    out_ref[...] = total.astype(jnp.bfloat16)


def call(kernel, out_shape, specs, *args, scratch=(), flops=0, out_dtype=jnp.bfloat16, vmem=16):
    shapes = out_shape if isinstance(out_shape, list) else [out_shape]
    size = sum(a.size * a.dtype.itemsize for a in args)
    size += sum(math.prod(shape) * jnp.dtype(out_dtype).itemsize for shape in shapes)
    results = pl.pallas_call(
        kernel,
        out_shape=[jax.ShapeDtypeStruct(shape, out_dtype) for shape in shapes],
        in_specs=specs,
        out_specs=[VMEM] * len(shapes),
        scratch_shapes=scratch,
        compiler_params=pltpu.CompilerParams(vmem_limit_bytes=vmem << 20),
        cost_estimate=pl.CostEstimate(flops=flops, bytes_accessed=size, transcendentals=0),
    )(*args)
    return results if isinstance(out_shape, list) else results[0]


def body(queries, keys, values, head_class, window_lengths, out_weight):
    core = lax.axis_index("core")
    group = lax.axis_index("head").astype(jnp.int32).reshape(1)
    width = TOK // FRAMES
    weight = lax.all_gather(out_weight, Z_AXES, axis=0, tiled=False)
    weight = call(rows_kernel, (320, 2 * COLS), [VMEM], weight)
    around = [
        lax.ppermute(weight, "x", [((x + step) % 4, x) for x in range(4)]) for step in (1, 3, 2)
    ]
    after, weight = lax.optimization_barrier((group, weight))
    packed = call(
        pack_kernel,
        (TOK, 3 * TMAX * HD),
        [SMEM] * 2 + [VMEM] * 3,
        after,
        head_class,
        queries,
        keys,
        values,
    )
    packed, window_lengths = lax.optimization_barrier((packed, window_lengths))
    packed = lax.all_to_all(
        packed.reshape(FRAMES, width, 3 * TMAX * HD), FRAME_AXES, 0, 0, tiled=True
    ).reshape(TOK, 3 * TMAX * HD)
    spatial = call(
        window_kernel, (TOK, COLS), [SMEM] + [VMEM] * 3, window_lengths, queries, keys, values
    )
    packed, spatial = lax.optimization_barrier((packed, spatial))
    attended, mark = call(frame_kernel, [(TOK, TMAX * HD), (16, HD)], [VMEM], packed)
    mark, weight = lax.optimization_barrier((mark, weight))
    mark, last = lax.optimization_barrier((mark, around[2]))
    mark, middle = lax.optimization_barrier((mark, around[1]))
    mark, first = lax.optimization_barrier((mark, around[0]))
    around = [first, middle, last]
    swap = [(0, 1), (1, 0)]
    slabs = [weight, *around]
    slabs = slabs + [lax.ppermute(slab, "core", swap) for slab in slabs]
    attended = lax.all_to_all(
        attended.reshape(FRAMES, width, TMAX * HD), FRAME_AXES, 0, 0, tiled=True
    ).reshape(TOK, TMAX * HD)

    source = jnp.arange(COLS, dtype=jnp.int32)[:, None]
    place = jnp.arange(COLS, dtype=jnp.int32)[None, :]
    turn = place // 80 % 4
    turn = turn + (turn == 2) - (turn == 3)
    owner = (lax.axis_index("x") + turn) % 4 * 2 + (core + place // 320) % 2
    wanted = place % 80 // 20 * 160 + owner * 20 + place % 20
    order = (source == wanted).astype(jnp.bfloat16)
    mixed = call(
        mix_kernel,
        (4, TOK, COLS),
        [SMEM] * 2 + [VMEM] * 3,
        group,
        head_class,
        spatial,
        attended,
        order,
        scratch=[pltpu.VMEM((TOK, COLS), jnp.bfloat16)],
    )
    mixed = lax.all_to_all(mixed, "head", 0, 0, tiled=True)
    return call(
        project_kernel,
        (TOK, 2 * COLS),
        [VMEM] * 10,
        mixed,
        mark,
        *slabs,
        flops=2 * TOK * 2560 * 1280,
    )


def solution(mesh):
    mesh = Mesh(mesh.devices.reshape(4, 2, 2, 4, 2, 4), TOKEN_AXES + ("head",))
    split = P(TOKEN_AXES, "head")
    placed = (split, split, split, P(), P(TOKEN_AXES, None), split)
    return jax.shard_map(body, mesh=mesh, in_specs=placed, out_specs=split, check_vma=False)
```

```python
import functools
import math

import jax
import jax.numpy as jnp
from jax import lax
from jax.experimental import pallas as pl
from jax.experimental.pallas import tpu as pltpu
from jax.sharding import Mesh, PartitionSpec as P

HD = 128
TMAX = 3
FRAMES = 8
TOK = 128
LOCAL = 5
COLS = LOCAL * HD
SCALE = 1.0 / math.sqrt(HD)
FRAME_AXES = ("far", "near")
Z_AXES = ("far", "near", "half")
TOKEN_AXES = Z_AXES + ("x", "core")
VMEM = pl.BlockSpec(memory_space=pltpu.VMEM)
SMEM = pl.BlockSpec(memory_space=pltpu.SMEM)
HBM = pl.BlockSpec(memory_space=pltpu.HBM)


def columns(head):
    return pl.ds(pl.multiple_of(head * HD, HD), HD)


def ranks(classes_ref, group):
    found, before = [], 0
    for head in range(LOCAL):
        temporal = classes_ref[group * LOCAL + head] == 1
        found.append((temporal, before))
        before = before + temporal.astype(jnp.int32)
    return found


def pack_kernel(group_ref, classes_ref, q_ref, k_ref, v_ref, out_ref):
    slots = [0] * TMAX
    for head, (temporal, before) in enumerate(ranks(classes_ref, group_ref[0])):
        slots = [
            jnp.where(temporal & (before == slot), head, taken)
            for slot, taken in enumerate(slots)
        ]
    for part, source in enumerate((q_ref, k_ref, v_ref)):
        for slot in range(TMAX):
            place = (part * TMAX + slot) * HD
            out_ref[:, place : place + HD] = source[:, columns(slots[slot])]


def attend(query, key, value, same):
    scores = lax.dot_general(
        query, key, (((1,), (1,)), ((), ())), preferred_element_type=jnp.float32
    )
    scores = jnp.where(same, scores * SCALE, -1e30)
    weights = jnp.exp(scores - jnp.max(scores, axis=-1, keepdims=True))
    weights = weights / jnp.sum(weights, axis=-1, keepdims=True)
    return jnp.dot(
        weights.astype(jnp.bfloat16), value, preferred_element_type=jnp.float32
    ).astype(jnp.bfloat16)


def window_kernel(lengths_ref, q_ref, k_ref, v_ref, out_ref):
    rows = lax.broadcasted_iota(jnp.int32, (TOK, TOK), 0)
    cols = lax.broadcasted_iota(jnp.int32, (TOK, TOK), 1)
    row_id = jnp.zeros((TOK, TOK), jnp.int32)
    col_id = jnp.zeros((TOK, TOK), jnp.int32)
    end = 0
    for window in range(4):
        end = end + lengths_ref[0, window]
        row_id = row_id + (rows >= end).astype(jnp.int32)
        col_id = col_id + (cols >= end).astype(jnp.int32)
    same = row_id == col_id
    for head in range(LOCAL):
        span = slice(head * HD, (head + 1) * HD)
        out_ref[:, span] = attend(q_ref[:, span], k_ref[:, span], v_ref[:, span], same)


def frame_kernel(packed_ref, out_ref, mark_ref):
    width = TOK // FRAMES
    rows = lax.broadcasted_iota(jnp.int32, (TOK, TOK), 0)
    cols = lax.broadcasted_iota(jnp.int32, (TOK, TOK), 1)
    same = (rows & (width - 1)) == (cols & (width - 1))
    mark_ref[...] = packed_ref[:16, :HD]
    for slot in range(TMAX):
        span = [
            slice((part * TMAX + slot) * HD, (part * TMAX + slot + 1) * HD) for part in range(3)
        ]
        out_ref[:, slot * HD : (slot + 1) * HD] = attend(
            packed_ref[:, span[0]], packed_ref[:, span[1]], packed_ref[:, span[2]], same
        )


def mix_kernel(group_ref, classes_ref, spatial_ref, temporal_ref, order_ref, out_ref, mixed):
    for head, (temporal, before) in enumerate(ranks(classes_ref, group_ref[0])):
        span = slice(head * HD, (head + 1) * HD)

        @pl.when(jnp.logical_not(temporal))
        def _():
            mixed[:, span] = spatial_ref[:, span]

        @pl.when(temporal)
        def _():
            mixed[:, span] = temporal_ref[:, columns(before)]

    ordered = jnp.dot(mixed[...], order_ref[...], preferred_element_type=jnp.float32)
    ordered = ordered.astype(jnp.bfloat16)
    out_ref[...] = ordered


def rows_kernel(weight_ref, out_ref):
    for group in range(4):
        out_ref[group * 80 : (group + 1) * 80, :] = jnp.concatenate(
            [weight_ref[4 * group + z] for z in range(4)], axis=0
        )


def project_kernel(mixed_ref, mark_ref, *refs):
    slabs, out_ref = refs[:8], refs[8]
    total = jnp.zeros((TOK, 2 * COLS), jnp.float32)
    for group in range(4):
        rows = [slab[group * 80 : (group + 1) * 80, :] for slab in slabs]
        total = total + jnp.dot(
            mixed_ref[group],
            jnp.concatenate(rows, axis=0),
            preferred_element_type=jnp.float32,
        )
    out_ref[...] = total.astype(jnp.bfloat16)


def call(kernel, out_shape, specs, *args, scratch=(), flops=0, out_dtype=jnp.bfloat16, vmem=16):
    shapes = out_shape if isinstance(out_shape, list) else [out_shape]
    size = sum(a.size * a.dtype.itemsize for a in args)
    size += sum(math.prod(shape) * jnp.dtype(out_dtype).itemsize for shape in shapes)
    results = pl.pallas_call(
        kernel,
        out_shape=[jax.ShapeDtypeStruct(shape, out_dtype) for shape in shapes],
        in_specs=specs,
        out_specs=[VMEM] * len(shapes),
        scratch_shapes=scratch,
        compiler_params=pltpu.CompilerParams(vmem_limit_bytes=vmem << 20),
        cost_estimate=pl.CostEstimate(flops=flops, bytes_accessed=size, transcendentals=0),
    )(*args)
    return results if isinstance(out_shape, list) else results[0]


def body(queries, keys, values, head_class, window_lengths, out_weight):
    core = lax.axis_index("core")
    group = lax.axis_index("head").astype(jnp.int32).reshape(1)
    width = TOK // FRAMES
    weight = lax.all_gather(out_weight, Z_AXES, axis=0, tiled=False)
    weight = call(rows_kernel, (320, 2 * COLS), [VMEM], weight)
    around = [
        lax.ppermute(weight, "x", [((x + step) % 4, x) for x in range(4)]) for step in (1, 3, 2)
    ]
    after, weight = lax.optimization_barrier((group, weight))
    packed = call(
        pack_kernel,
        (TOK, 3 * TMAX * HD),
        [SMEM] * 2 + [VMEM] * 3,
        after,
        head_class,
        queries,
        keys,
        values,
    )
    packed = lax.all_to_all(
        packed.reshape(FRAMES, width, 3 * TMAX * HD), FRAME_AXES, 0, 0, tiled=True
    ).reshape(TOK, 3 * TMAX * HD)
    attended, mark = call(frame_kernel, [(TOK, TMAX * HD), (16, HD)], [VMEM], packed)
    mark, weight = lax.optimization_barrier((mark, weight))
    mark, window_lengths = lax.optimization_barrier((mark, window_lengths))
    spatial = call(
        window_kernel, (TOK, COLS), [SMEM] + [VMEM] * 3, window_lengths, queries, keys, values
    )
    spatial, last = lax.optimization_barrier((spatial, around[2]))
    spatial, middle = lax.optimization_barrier((spatial, around[1]))
    spatial, first = lax.optimization_barrier((spatial, around[0]))
    around = [first, middle, last]
    swap = [(0, 1), (1, 0)]
    slabs = [weight, *around]
    slabs = slabs + [lax.ppermute(slab, "core", swap) for slab in slabs]
    attended = lax.all_to_all(
        attended.reshape(FRAMES, width, TMAX * HD), FRAME_AXES, 0, 0, tiled=True
    ).reshape(TOK, TMAX * HD)

    source = jnp.arange(COLS, dtype=jnp.int32)[:, None]
    place = jnp.arange(COLS, dtype=jnp.int32)[None, :]
    turn = place // 80 % 4
    turn = turn + (turn == 2) - (turn == 3)
    owner = (lax.axis_index("x") + turn) % 4 * 2 + (core + place // 320) % 2
    wanted = place % 80 // 20 * 160 + owner * 20 + place % 20
    order = (source == wanted).astype(jnp.bfloat16)
    mixed = call(
        mix_kernel,
        (TOK, COLS),
        [SMEM] * 2 + [VMEM] * 3,
        group,
        head_class,
        spatial,
        attended,
        order,
        scratch=[pltpu.VMEM((TOK, COLS), jnp.bfloat16)],
    )
    mixed = lax.all_gather(mixed, "head", axis=0, tiled=False)
    mark = mark + mixed[0, :16, :HD]
    return call(
        project_kernel,
        (TOK, 2 * COLS),
        [VMEM] * 10,
        mixed,
        mark,
        *slabs,
        flops=2 * TOK * 2560 * 1280,
    )


def solution(mesh):
    mesh = Mesh(mesh.devices.reshape(4, 2, 2, 4, 2, 4), TOKEN_AXES + ("head",))
    split = P(TOKEN_AXES, "head")
    placed = (split, split, split, P(), P(TOKEN_AXES, None), split)
    return jax.shard_map(body, mesh=mesh, in_specs=placed, out_specs=split, check_vma=False)
```

```python
import functools
import math

import jax
import jax.numpy as jnp
from jax import lax
from jax.experimental import pallas as pl
from jax.experimental.pallas import tpu as pltpu
from jax.sharding import Mesh, PartitionSpec as P

HD = 128
TMAX = 3
FRAMES = 8
TOK = 128
LOCAL = 5
COLS = LOCAL * HD
SCALE = 1.0 / math.sqrt(HD)
FRAME_AXES = ("far", "near")
Z_AXES = ("far", "near", "half")
TOKEN_AXES = Z_AXES + ("x", "core")
VMEM = pl.BlockSpec(memory_space=pltpu.VMEM)
SMEM = pl.BlockSpec(memory_space=pltpu.SMEM)
HBM = pl.BlockSpec(memory_space=pltpu.HBM)


def columns(head):
    return pl.ds(pl.multiple_of(head * HD, HD), HD)


def ranks(classes_ref, group):
    found, before = [], 0
    for head in range(LOCAL):
        temporal = classes_ref[group * LOCAL + head] == 1
        found.append((temporal, before))
        before = before + temporal.astype(jnp.int32)
    return found


def pack_kernel(group_ref, classes_ref, q_ref, k_ref, v_ref, out_ref):
    slots = [0] * TMAX
    for head, (temporal, before) in enumerate(ranks(classes_ref, group_ref[0])):
        slots = [
            jnp.where(temporal & (before == slot), head, taken)
            for slot, taken in enumerate(slots)
        ]
    for part, source in enumerate((q_ref, k_ref, v_ref)):
        for slot in range(TMAX):
            place = (part * TMAX + slot) * HD
            out_ref[:, place : place + HD] = source[:, columns(slots[slot])]


def attend(query, key, value, same):
    scores = lax.dot_general(
        query, key, (((1,), (1,)), ((), ())), preferred_element_type=jnp.float32
    )
    scores = jnp.where(same, scores * SCALE, -1e30)
    weights = jnp.exp(scores - jnp.max(scores, axis=-1, keepdims=True))
    weights = weights / jnp.sum(weights, axis=-1, keepdims=True)
    return jnp.dot(
        weights.astype(jnp.bfloat16), value, preferred_element_type=jnp.float32
    ).astype(jnp.bfloat16)


def window_kernel(lengths_ref, q_ref, k_ref, v_ref, out_ref):
    rows = lax.broadcasted_iota(jnp.int32, (TOK, TOK), 0)
    cols = lax.broadcasted_iota(jnp.int32, (TOK, TOK), 1)
    row_id = jnp.zeros((TOK, TOK), jnp.int32)
    col_id = jnp.zeros((TOK, TOK), jnp.int32)
    end = 0
    for window in range(4):
        end = end + lengths_ref[0, window]
        row_id = row_id + (rows >= end).astype(jnp.int32)
        col_id = col_id + (cols >= end).astype(jnp.int32)
    same = row_id == col_id
    for head in range(LOCAL):
        span = slice(head * HD, (head + 1) * HD)
        out_ref[:, span] = attend(q_ref[:, span], k_ref[:, span], v_ref[:, span], same)


def frame_kernel(packed_ref, out_ref, mark_ref):
    width = TOK // FRAMES
    rows = lax.broadcasted_iota(jnp.int32, (TOK, TOK), 0)
    cols = lax.broadcasted_iota(jnp.int32, (TOK, TOK), 1)
    same = (rows & (width - 1)) == (cols & (width - 1))
    mark_ref[...] = packed_ref[:16, :HD]
    for slot in range(TMAX):
        span = [
            slice((part * TMAX + slot) * HD, (part * TMAX + slot + 1) * HD) for part in range(3)
        ]
        out_ref[:, slot * HD : (slot + 1) * HD] = attend(
            packed_ref[:, span[0]], packed_ref[:, span[1]], packed_ref[:, span[2]], same
        )


def mix_kernel(group_ref, classes_ref, spatial_ref, temporal_ref, order_ref, out_ref, mixed):
    for head, (temporal, before) in enumerate(ranks(classes_ref, group_ref[0])):
        span = slice(head * HD, (head + 1) * HD)

        @pl.when(jnp.logical_not(temporal))
        def _():
            mixed[:, span] = spatial_ref[:, span]

        @pl.when(temporal)
        def _():
            mixed[:, span] = temporal_ref[:, columns(before)]

    ordered = jnp.dot(mixed[...], order_ref[...], preferred_element_type=jnp.float32)
    ordered = ordered.astype(jnp.bfloat16)
    out_ref[...] = ordered


def rows_kernel(weight_ref, out_ref):
    for group in range(4):
        out_ref[group * 80 : (group + 1) * 80, :] = jnp.concatenate(
            [weight_ref[4 * group + z] for z in range(4)], axis=0
        )


def project_kernel(mixed_ref, mark_ref, *refs):
    slabs, (out_ref, total) = refs[:8], refs[8:]
    group = pl.program_id(0)
    product = jnp.dot(
        mixed_ref[0],
        jnp.concatenate([slab[...] for slab in slabs], axis=0),
        preferred_element_type=jnp.float32,
    )

    @pl.when(group == 0)
    def _():
        total[...] = product

    @pl.when(group > 0)
    def _():
        total[...] += product

    @pl.when(group == 3)
    def _():
        out_ref[...] = total[...].astype(jnp.bfloat16)


def call(kernel, out_shape, specs, *args, scratch=(), flops=0, out_dtype=jnp.bfloat16, vmem=16, grid=(), out_specs=None):
    shapes = out_shape if isinstance(out_shape, list) else [out_shape]
    size = sum(a.size * a.dtype.itemsize for a in args)
    size += sum(math.prod(shape) * jnp.dtype(out_dtype).itemsize for shape in shapes)
    results = pl.pallas_call(
        kernel,
        grid=grid,
        out_shape=[jax.ShapeDtypeStruct(shape, out_dtype) for shape in shapes],
        in_specs=specs,
        out_specs=out_specs or [VMEM] * len(shapes),
        scratch_shapes=scratch,
        compiler_params=pltpu.CompilerParams(vmem_limit_bytes=vmem << 20),
        cost_estimate=pl.CostEstimate(flops=flops, bytes_accessed=size, transcendentals=0),
    )(*args)
    return results if isinstance(out_shape, list) else results[0]


def body(queries, keys, values, head_class, window_lengths, out_weight):
    core = lax.axis_index("core")
    group = lax.axis_index("head").astype(jnp.int32).reshape(1)
    width = TOK // FRAMES
    weight = lax.all_gather(out_weight, Z_AXES, axis=0, tiled=False)
    weight = call(rows_kernel, (320, 2 * COLS), [VMEM], weight)
    around = [
        lax.ppermute(weight, "x", [((x + step) % 4, x) for x in range(4)]) for step in (1, 3, 2)
    ]
    after, weight = lax.optimization_barrier((group, weight))
    packed = call(
        pack_kernel,
        (TOK, 3 * TMAX * HD),
        [SMEM] * 2 + [VMEM] * 3,
        after,
        head_class,
        queries,
        keys,
        values,
    )
    packed = lax.all_to_all(
        packed.reshape(FRAMES, width, 3 * TMAX * HD), FRAME_AXES, 0, 0, tiled=True
    ).reshape(TOK, 3 * TMAX * HD)
    attended, mark = call(frame_kernel, [(TOK, TMAX * HD), (16, HD)], [VMEM], packed)
    mark, weight = lax.optimization_barrier((mark, weight))
    mark, window_lengths = lax.optimization_barrier((mark, window_lengths))
    spatial = call(
        window_kernel, (TOK, COLS), [SMEM] + [VMEM] * 3, window_lengths, queries, keys, values
    )
    spatial, last = lax.optimization_barrier((spatial, around[2]))
    spatial, middle = lax.optimization_barrier((spatial, around[1]))
    spatial, first = lax.optimization_barrier((spatial, around[0]))
    around = [first, middle, last]
    swap = [(0, 1), (1, 0)]
    slabs = [weight, *around]
    slabs = slabs + [lax.ppermute(slab, "core", swap) for slab in slabs]
    attended = lax.all_to_all(
        attended.reshape(FRAMES, width, TMAX * HD), FRAME_AXES, 0, 0, tiled=True
    ).reshape(TOK, TMAX * HD)

    source = jnp.arange(COLS, dtype=jnp.int32)[:, None]
    place = jnp.arange(COLS, dtype=jnp.int32)[None, :]
    turn = place // 80 % 4
    turn = turn + (turn == 2) - (turn == 3)
    owner = (lax.axis_index("x") + turn) % 4 * 2 + (core + place // 320) % 2
    wanted = place % 80 // 20 * 160 + owner * 20 + place % 20
    order = (source == wanted).astype(jnp.bfloat16)
    mixed = call(
        mix_kernel,
        (TOK, COLS),
        [SMEM] * 2 + [VMEM] * 3,
        group,
        head_class,
        spatial,
        attended,
        order,
        scratch=[pltpu.VMEM((TOK, COLS), jnp.bfloat16)],
    )
    mixed = lax.all_gather(mixed, "head", axis=0, tiled=False)
    mark = mark + mixed[0, :16, :HD]
    return call(
        project_kernel,
        (TOK, 2 * COLS),
        [
            pl.BlockSpec((1, TOK, COLS), lambda group: (group, 0, 0)),
            pl.BlockSpec((16, HD), lambda group: (0, 0)),
        ]
        + [pl.BlockSpec((80, 2 * COLS), lambda group: (group, 0))] * 8,
        mixed,
        mark,
        *slabs,
        grid=(4,),
        out_specs=[pl.BlockSpec((TOK, 2 * COLS), lambda group: (0, 0))],
        scratch=[pltpu.VMEM((TOK, 2 * COLS), jnp.float32)],
        flops=2 * TOK * 2560 * 1280,
    )


def solution(mesh):
    mesh = Mesh(mesh.devices.reshape(4, 2, 2, 4, 2, 4), TOKEN_AXES + ("head",))
    split = P(TOKEN_AXES, "head")
    placed = (split, split, split, P(), P(TOKEN_AXES, None), split)
    return jax.shard_map(body, mesh=mesh, in_specs=placed, out_specs=split, check_vma=False)
```

```python
import functools
import math

import jax
import jax.numpy as jnp
from jax import lax
from jax.experimental import pallas as pl
from jax.experimental.pallas import tpu as pltpu
from jax.sharding import Mesh, PartitionSpec as P

HD = 128
TMAX = 3
FRAMES = 8
TOK = 128
LOCAL = 5
COLS = LOCAL * HD
SCALE = 1.0 / math.sqrt(HD)
FRAME_AXES = ("far", "near")
Z_AXES = ("far", "near", "half")
TOKEN_AXES = Z_AXES + ("x", "core")
VMEM = pl.BlockSpec(memory_space=pltpu.VMEM)
SMEM = pl.BlockSpec(memory_space=pltpu.SMEM)
HBM = pl.BlockSpec(memory_space=pltpu.HBM)


def columns(head):
    return pl.ds(pl.multiple_of(head * HD, HD), HD)


def ranks(classes_ref, group):
    found, before = [], 0
    for head in range(LOCAL):
        temporal = classes_ref[group * LOCAL + head] == 1
        found.append((temporal, before))
        before = before + temporal.astype(jnp.int32)
    return found


def pack_kernel(group_ref, classes_ref, q_ref, k_ref, v_ref, out_ref):
    slots = [0] * TMAX
    for head, (temporal, before) in enumerate(ranks(classes_ref, group_ref[0])):
        slots = [
            jnp.where(temporal & (before == slot), head, taken)
            for slot, taken in enumerate(slots)
        ]
    for part, source in enumerate((q_ref, k_ref, v_ref)):
        for slot in range(TMAX):
            place = (part * TMAX + slot) * HD
            out_ref[:, place : place + HD] = source[:, columns(slots[slot])]


def attend(query, key, value, same):
    scores = lax.dot_general(
        query, key, (((1,), (1,)), ((), ())), preferred_element_type=jnp.float32
    )
    scores = jnp.where(same, scores * SCALE, -1e30)
    weights = jnp.exp(scores - jnp.max(scores, axis=-1, keepdims=True))
    weights = weights / jnp.sum(weights, axis=-1, keepdims=True)
    return jnp.dot(
        weights.astype(jnp.bfloat16), value, preferred_element_type=jnp.float32
    ).astype(jnp.bfloat16)


def window_kernel(lengths_ref, q_ref, k_ref, v_ref, out_ref):
    rows = lax.broadcasted_iota(jnp.int32, (TOK, TOK), 0)
    cols = lax.broadcasted_iota(jnp.int32, (TOK, TOK), 1)
    row_id = jnp.zeros((TOK, TOK), jnp.int32)
    col_id = jnp.zeros((TOK, TOK), jnp.int32)
    end = 0
    for window in range(4):
        end = end + lengths_ref[0, window]
        row_id = row_id + (rows >= end).astype(jnp.int32)
        col_id = col_id + (cols >= end).astype(jnp.int32)
    same = row_id == col_id
    for head in range(LOCAL):
        span = slice(head * HD, (head + 1) * HD)
        out_ref[:, span] = attend(q_ref[:, span], k_ref[:, span], v_ref[:, span], same)


def frame_kernel(packed_ref, out_ref, mark_ref):
    width = TOK // FRAMES
    rows = lax.broadcasted_iota(jnp.int32, (TOK, TOK), 0)
    cols = lax.broadcasted_iota(jnp.int32, (TOK, TOK), 1)
    same = (rows & (width - 1)) == (cols & (width - 1))
    mark_ref[...] = packed_ref[:16, :HD]
    for slot in range(TMAX):
        span = [
            slice((part * TMAX + slot) * HD, (part * TMAX + slot + 1) * HD) for part in range(3)
        ]
        out_ref[:, slot * HD : (slot + 1) * HD] = attend(
            packed_ref[:, span[0]], packed_ref[:, span[1]], packed_ref[:, span[2]], same
        )


def mix_kernel(group_ref, classes_ref, spatial_ref, temporal_ref, order_ref, out_ref, mixed):
    for head, (temporal, before) in enumerate(ranks(classes_ref, group_ref[0])):
        span = slice(head * HD, (head + 1) * HD)

        @pl.when(jnp.logical_not(temporal))
        def _():
            mixed[:, span] = spatial_ref[:, span]

        @pl.when(temporal)
        def _():
            mixed[:, span] = temporal_ref[:, columns(before)]

    ordered = jnp.dot(mixed[...], order_ref[...], preferred_element_type=jnp.float32)
    ordered = ordered.astype(jnp.bfloat16)
    out_ref[...] = ordered


def rows_kernel(weight_ref, out_ref):
    for group in range(4):
        out_ref[group * 80 : (group + 1) * 80, :] = jnp.concatenate(
            [weight_ref[4 * group + z] for z in range(4)], axis=0
        )


def project_kernel(mixed_ref, mark_ref, *refs):
    slabs, out_ref = refs[:8], refs[8]
    total = jnp.zeros((TOK, 2 * COLS), jnp.float32)
    for group in range(4):
        rows = [slab[group * 80 : (group + 1) * 80, :] for slab in slabs]
        total = total + jnp.dot(
            mixed_ref[group],
            jnp.concatenate(rows, axis=0),
            preferred_element_type=jnp.float32,
        )
    out_ref[...] = total.astype(jnp.bfloat16)


def call(kernel, out_shape, specs, *args, scratch=(), flops=0, out_dtype=jnp.bfloat16, vmem=16):
    shapes = out_shape if isinstance(out_shape, list) else [out_shape]
    size = sum(a.size * a.dtype.itemsize for a in args)
    size += sum(math.prod(shape) * jnp.dtype(out_dtype).itemsize for shape in shapes)
    results = pl.pallas_call(
        kernel,
        out_shape=[jax.ShapeDtypeStruct(shape, out_dtype) for shape in shapes],
        in_specs=specs,
        out_specs=[VMEM] * len(shapes),
        scratch_shapes=scratch,
        compiler_params=pltpu.CompilerParams(vmem_limit_bytes=vmem << 20),
        cost_estimate=pl.CostEstimate(flops=flops, bytes_accessed=size, transcendentals=0),
    )(*args)
    return results if isinstance(out_shape, list) else results[0]


def body(queries, keys, values, head_class, window_lengths, out_weight):
    core = lax.axis_index("core")
    group = lax.axis_index("head").astype(jnp.int32).reshape(1)
    width = TOK // FRAMES
    weight = lax.all_gather(out_weight, Z_AXES, axis=0, tiled=False)
    weight = call(rows_kernel, (320, 2 * COLS), [VMEM], weight)
    around = [
        lax.ppermute(weight, "x", [((x + step) % 4, x) for x in range(4)]) for step in (1, 3, 2)
    ]
    after, weight = lax.optimization_barrier((group, weight))
    packed = call(
        pack_kernel,
        (TOK, 3 * TMAX * HD),
        [SMEM] * 2 + [VMEM] * 3,
        after,
        head_class,
        queries,
        keys,
        values,
    )
    packed = lax.all_to_all(
        packed.reshape(FRAMES, width, 3 * TMAX * HD), FRAME_AXES, 0, 0, tiled=True
    ).reshape(TOK, 3 * TMAX * HD)
    attended, mark = call(frame_kernel, [(TOK, TMAX * HD), (16, HD)], [VMEM], packed)
    mark, weight = lax.optimization_barrier((mark, weight))
    source = jnp.arange(COLS, dtype=jnp.int32)[:, None]
    place = jnp.arange(COLS, dtype=jnp.int32)[None, :]
    turn = place // 80 % 4
    turn = turn + (turn == 2) - (turn == 3)
    owner = (lax.axis_index("x") + turn) % 4 * 2 + (core + place // 320) % 2
    wanted = place % 80 // 20 * 160 + owner * 20 + place % 20
    order = (source == wanted).astype(jnp.bfloat16)
    mark, window_lengths, order = lax.optimization_barrier((mark, window_lengths, order))
    spatial = call(
        window_kernel, (TOK, COLS), [SMEM] + [VMEM] * 3, window_lengths, queries, keys, values
    )
    spatial, last = lax.optimization_barrier((spatial, around[2]))
    spatial, middle = lax.optimization_barrier((spatial, around[1]))
    spatial, first = lax.optimization_barrier((spatial, around[0]))
    around = [first, middle, last]
    swap = [(0, 1), (1, 0)]
    slabs = [weight, *around]
    slabs = slabs + [lax.ppermute(slab, "core", swap) for slab in slabs]
    attended = lax.all_to_all(
        attended.reshape(FRAMES, width, TMAX * HD), FRAME_AXES, 0, 0, tiled=True
    ).reshape(TOK, TMAX * HD)

    mixed = call(
        mix_kernel,
        (TOK, COLS),
        [SMEM] * 2 + [VMEM] * 3,
        group,
        head_class,
        spatial,
        attended,
        order,
        scratch=[pltpu.VMEM((TOK, COLS), jnp.bfloat16)],
    )
    mixed = lax.all_gather(mixed, "head", axis=0, tiled=False)
    mark = mark + mixed[0, :16, :HD]
    return call(
        project_kernel,
        (TOK, 2 * COLS),
        [VMEM] * 10,
        mixed,
        mark,
        *slabs,
        flops=2 * TOK * 2560 * 1280,
    )


def solution(mesh):
    mesh = Mesh(mesh.devices.reshape(4, 2, 2, 4, 2, 4), TOKEN_AXES + ("head",))
    split = P(TOKEN_AXES, "head")
    placed = (split, split, split, P(), P(TOKEN_AXES, None), split)
    return jax.shard_map(body, mesh=mesh, in_specs=placed, out_specs=split, check_vma=False)
```
